32 devices in a mesh: group: 2 (over x), frame: 16 (over z, y, core).
Axes of the slice: x: 2, y: 2, z: 4, core: 2. Of those that a mesh axis runs over, the one named last changes fastest.
Arguments:
- queries: bfloat16 [10240, 5120], P(('group', 'frame')), parts along dimension 0, may hold values from -33 to 33
- keys: bfloat16 [10240, 5120], P(('group', 'frame')), parts along dimension 0, may hold values from -33 to 33
- values: bfloat16 [10240, 5120], P(('group', 'frame')), parts along dimension 0, may hold values from -6 to 6
- labels: int32 [80], P('group'), parts along dimension 0, may hold values from 0 to 1, as said below
- band: int32 [80], P('group'), parts along dimension 0, may hold values from 2 to 4
Outputs:
- attended: bfloat16 [10240, 5120], P(('group', 'frame')), parts along dimension 0
The draws below stay inside these ranges and needn't reach their ends.
There are 2 independent parts, one for each index of `group`. The reference program is written for one: setup_inputs(seed, part) draws one part's arguments, and reference() takes and returns one part's arrays. A program takes and returns all parts, laid end to end along the dimension named above; each array names one. Nothing has to cross between parts.
Inputs may be any that keep to these rules, and one draw needn't show every extreme that they name: `labels`: exactly 10 of the 40 heads carry 1, the others 0.
All inputs are finite; a program needn't handle non-finite values.
Results may differ from the reference program's by a relative error of at most 0.0049.
Values may be sent and summed in bfloat16 or wider, within the bound.
A program may use at most 128 MiB of HBM per device.

```python
import math
import jax
import jax.numpy as jnp
from jax import lax

HEADS = 40
HEAD_DIM = 128
TEMP_HEADS = 10
FRAMES = 8
FPIX = 640
TOKENS = 5120
WIDTH = 5120


def drawn_rows(key):
    return jnp.clip(jax.random.normal(key, (TOKENS, HEADS * HEAD_DIM), jnp.float32), -6.0, 6.0)


def draw_queries(key, part):
    result = drawn_rows(jax.random.fold_in(key, 1))
    return result.astype(jnp.bfloat16)


def draw_keys(key, part):
    result = drawn_rows(jax.random.fold_in(key, 2))
    return result.astype(jnp.bfloat16)


def draw_labels(key, part):
    order = jax.random.permutation(key, HEADS)
    return (order < TEMP_HEADS).astype(jnp.int32)


def set_ends(array, key, smallest, largest):
    extent = array.shape
    spot = [jax.random.randint(jax.random.fold_in(key, axis), (), 0, extent[axis]) for axis in range(len(extent))]
    array = array.at[tuple(spot)].set(smallest)
    longest = extent.index(max(extent))
    spot[longest] = (spot[longest] + 1) % extent[longest]
    return array.at[tuple(spot)].set(largest)


def block_scale(stream_key, dims, cuts, low, top_value):
    gain = 1.0
    for axis_at, blocks in cuts:
        heights = jax.random.uniform(jax.random.fold_in(jax.random.fold_in(stream_key, 6), axis_at), (blocks,), jnp.float32, low / len(cuts), top_value / len(cuts))
        gain = gain * jnp.repeat(jnp.exp(heights), dims[axis_at] // blocks).reshape((-1,) + (1,) * (len(dims) - 1 - axis_at))
    return gain


def normal_values(stream_key, dims, width, reach, cuts=(), held_as=jnp.bfloat16):
    factor_of = block_scale(stream_key, dims, cuts, -0.22, 0.18) if cuts else 1.0
    values = jax.random.normal(stream_key, dims, jnp.float32) * width * factor_of
    return jnp.minimum(jnp.maximum(values, -reach), reach).astype(held_as)


def setup_inputs(seed: int = 0, part: int = 0) -> dict:
    key_list = jax.random.split(jax.random.key(seed), 6)
    part_keys = jax.random.split(jax.random.fold_in(key_list[5], part), 6)
    queries = draw_queries(jax.random.fold_in(jax.random.fold_in(key_list[5], part), 71), part)
    keys = draw_keys(jax.random.fold_in(jax.random.fold_in(key_list[5], part), 71), part)
    values = normal_values(part_keys[2], (TOKENS, WIDTH), 1.0, 6.0, ((0, 16),))
    labels = draw_labels(jax.random.fold_in(jax.random.fold_in(key_list[5], part), 71), part)
    band = set_ends(jax.random.randint(part_keys[4], (HEADS,), FRAMES // 4, FRAMES // 2 + 1), jax.random.fold_in(part_keys[4], 1), FRAMES // 4, (FRAMES // 2 + 1) - 1).astype(jnp.int32)
    return dict(queries=queries, keys=keys, values=values, labels=labels, band=band)


def softmax_rounded(scores):
    peak = lax.optimization_barrier(jnp.max(scores, axis=-1, keepdims=True))
    weights = jnp.exp(scores - peak)
    return (weights / lax.optimization_barrier(jnp.sum(weights, axis=-1, keepdims=True))).astype(jnp.bfloat16)

def reference(queries, keys, values, labels, band):
    scale = 1.0 / math.sqrt(HEAD_DIM)
    grid_shape = (FRAMES, FPIX, HEADS, HEAD_DIM)
    query_grid = queries.reshape(grid_shape)
    key_grid = keys.reshape(grid_shape)
    value_grid = values.reshape(grid_shape)

    def one_frame(pieces):
        query_frame, key_frame, value_frame = pieces
        scores = jnp.einsum('phd,khd->hpk', query_frame.astype(jnp.float32), key_frame.astype(jnp.float32)) * scale
        weights = softmax_rounded(scores)
        return jnp.einsum('hpk,khd->phd', weights.astype(jnp.float32), value_frame.astype(jnp.float32)).astype(jnp.bfloat16)
    spatial = lax.map(one_frame, (query_grid, key_grid, value_grid))
    frame_ids = jnp.arange(FRAMES, dtype=jnp.int32)
    distance = jnp.abs(frame_ids[:, None] - frame_ids[None, :])

    def one_head(pieces):
        query_head, key_head, value_head, head_band = pieces
        keep = distance <= head_band
        scores = jnp.einsum('fpd,gpd->pfg', query_head.astype(jnp.float32), key_head.astype(jnp.float32)) * scale
        scores = jnp.where(keep[None], scores, jnp.float32(-1e+30))
        weights = softmax_rounded(scores)
        return jnp.einsum('pfg,gpd->fpd', weights.astype(jnp.float32), value_head.astype(jnp.float32)).astype(jnp.bfloat16)
    temporal = lax.map(one_head, (jnp.moveaxis(query_grid, 2, 0), jnp.moveaxis(key_grid, 2, 0), jnp.moveaxis(value_grid, 2, 0), band))
    temporal = jnp.moveaxis(temporal, 0, 2)
    chosen = jnp.where((labels == 1)[None, None, :, None], temporal, spatial)
    return chosen.reshape(TOKENS, HEADS * HEAD_DIM)
```

```python
import functools
import math

import jax
import jax.numpy as jnp
from jax import lax
from jax.experimental import pallas as pl
from jax.experimental.pallas import tpu as pltpu
from jax.sharding import PartitionSpec as P

TEMP_HEADS = 10
UNIT = 16
SIZE = 128
F32 = jnp.float32
BF16 = jnp.bfloat16


def temporal_positions(labels, heads):
    def pick(head, carry):
        count, found = carry
        label = labels[head]
        found = tuple(
            jnp.where(label * (count + 1) == slot + 1, head, have)
            for slot, have in enumerate(found)
        )
        return count + label, found

    zero = jnp.int32(0)
    return lax.fori_loop(0, heads, pick, (zero, (zero,) * TEMP_HEADS))[1]


def cut_units(units):
    first = (units + 1) // 2
    return [(0, first), (first, units - first)]


def attend(query, key, value, scale, keep=None):
    scores = lax.dot_general(query, key, (((1,), (1,)), ((), ())), preferred_element_type=F32)
    if keep is not None:
        scores = jnp.where(keep, scores, F32(-1e30))
    peak = jnp.max(scores, axis=1, keepdims=True)
    weights = jnp.exp2((scores - peak) * F32(scale * math.log2(math.e))).astype(BF16)
    wide = jnp.concatenate([value, jnp.ones_like(value)], axis=1)
    total = jnp.dot(weights, wide, preferred_element_type=F32)
    return (total[:, :SIZE] / total[:, SIZE:]).astype(BF16)


def kernel(
    frames,
    units,
    head_band,
    packed,
    q_hbm,
    k_hbm,
    v_hbm,
    spatial_hbm,
    temporal_hbm,
    q_own,
    k_all,
    v_all,
    got,
    result,
    spatial,
    load_sem,
    pair_send,
    pair_recv,
    own_sem,
    send_sem,
    recv_sem,
    back_own,
    back_send,
    back_recv,
    out_sem,
):
    rows, width = q_own.shape
    heads = width // SIZE
    groups = rows // UNIT
    share = units * UNIT
    scale = 1.0 / math.sqrt(SIZE)
    cuts = [(start * UNIT, count * UNIT) for start, count in cut_units(units)]
    me = lax.axis_index("frame")
    frame = me // 2
    core = me % 2
    partner = {"frame": me + 1 - 2 * core}

    def peer(other):
        return {"frame": other * 2 + core}

    own_rows = pl.ds(0, rows)
    loads = [
        pltpu.make_async_copy(q_hbm, q_own, load_sem.at[0]),
        pltpu.make_async_copy(k_hbm, k_all.at[own_rows], load_sem.at[1]),
        pltpu.make_async_copy(v_hbm, v_all.at[own_rows], load_sem.at[2]),
    ]
    for load in loads:
        load.start()

    barrier = pltpu.get_barrier_semaphore()
    pl.semaphore_signal(barrier, inc=1, device_id=partner, device_id_type=pl.DeviceIdType.MESH)

    def greet(step, _):
        pl.semaphore_signal(
            barrier,
            inc=1,
            device_id=peer((frame + step) % frames),
            device_id_type=pl.DeviceIdType.MESH,
        )
        return 0

    lax.fori_loop(1, frames, greet, 0)

    pl.semaphore_wait(barrier, frames)

    def part_copy(cut, tensor, to, source):
        first, count = cuts[cut]
        return pltpu.make_async_remote_copy(
            src_ref=packed.at[tensor, pl.ds(pl.multiple_of(to * share + first, UNIT), count)],
            dst_ref=got.at[tensor, frame, pl.ds(first, count)],
            send_sem=send_sem.at[cut, tensor, to],
            recv_sem=recv_sem.at[cut, tensor, source],
            device_id=peer(to),
            device_id_type=pl.DeviceIdType.MESH,
        )

    def own_copy(tensor):
        return pltpu.make_async_copy(
            packed.at[tensor, pl.ds(pl.multiple_of(frame * share, UNIT), share)],
            got.at[tensor, frame],
            own_sem.at[tensor],
        )

    def back_copy(cut, to, source):
        first, count = cuts[cut]
        return pltpu.make_async_remote_copy(
            src_ref=result.at[to, pl.ds(first, count)],
            dst_ref=temporal_hbm.at[pl.ds(pl.multiple_of(frame * share + first, UNIT), count)],
            send_sem=back_send.at[cut, to],
            recv_sem=back_recv.at[cut, source],
            device_id=peer(to),
            device_id_type=pl.DeviceIdType.MESH,
        )

    def back_own_copy(cut):
        first, count = cuts[cut]
        return pltpu.make_async_copy(
            result.at[frame, pl.ds(first, count)],
            temporal_hbm.at[pl.ds(pl.multiple_of(frame * share + first, UNIT), count)],
            back_own.at[cut],
        )

    def over_peers(action):
        def step_action(step, _):
            action((frame + step) % frames)
            return 0

        lax.fori_loop(1, frames, step_action, 0)

    pair = []
    for tensor, held in ((1, k_all), (2, v_all)):
        pair.append(
            pltpu.make_async_remote_copy(
                src_ref=held.at[own_rows],
                dst_ref=held.at[pl.ds(rows, rows)],
                send_sem=pair_send.at[tensor - 1],
                recv_sem=pair_recv.at[tensor - 1],
                device_id=partner,
                device_id_type=pl.DeviceIdType.MESH,
            )
        )

    for tensor in range(3):
        over_peers(lambda other, tensor=tensor: part_copy(0, tensor, other, frame).start())
        own_copy(tensor).start()
    for load in loads:
        load.wait()
    for copy in pair:
        copy.start()
    for cut in range(1, len(cuts)):
        for tensor in range(3):
            over_peers(
                lambda other, cut=cut, tensor=tensor: part_copy(cut, tensor, other, frame).start()
            )
    for copy in pair:
        copy.wait()

    def one_head(head, _):
        columns = pl.ds(pl.multiple_of(head * SIZE, SIZE), SIZE)
        spatial[:, columns] = attend(
            q_own[:, columns], k_all[:, columns], v_all[:, columns], scale
        )
        return 0

    lax.fori_loop(0, heads, one_head, 0)
    out_copy = pltpu.make_async_copy(spatial, spatial_hbm, out_sem)
    out_copy.start()

    for tensor in range(3):
        own_copy(tensor).wait()
    tall = frames * UNIT
    row_id = lax.broadcasted_iota(jnp.int32, (tall, tall), 0)
    column_id = lax.broadcasted_iota(jnp.int32, (tall, tall), 1)
    distance = jnp.where(
        row_id % UNIT == column_id % UNIT, jnp.abs(row_id // UNIT - column_id // UNIT), 2 * frames
    )
    for cut, (first, count) in enumerate(cuts):
        for tensor in range(3):
            over_peers(
                lambda other, cut=cut, tensor=tensor: part_copy(
                    cut, tensor, other, other
                ).wait_recv()
            )

        def one_unit(number, _, first=first):
            start = pl.multiple_of(first + number * UNIT, UNIT)
            place = frame * units + first // UNIT + number
            reach = head_band[jnp.minimum(place // groups, TEMP_HEADS - 1)]
            parts = [got[t, :, pl.ds(start, UNIT), :].reshape(tall, SIZE) for t in range(3)]
            out = attend(*parts, scale, distance <= reach)
            result[:, pl.ds(start, UNIT), :] = out.reshape(frames, UNIT, SIZE)
            return 0

        lax.fori_loop(0, count // UNIT, one_unit, 0)
        over_peers(lambda other, cut=cut: back_copy(cut, other, frame).start())
        back_own_copy(cut).start()

    for cut in range(len(cuts)):
        back_own_copy(cut).wait()
        over_peers(lambda other, cut=cut: back_copy(cut, other, other).wait())
        for tensor in range(3):
            over_peers(
                lambda other, cut=cut, tensor=tensor: part_copy(
                    cut, tensor, other, frame
                ).wait_send()
            )
    out_copy.wait()


def pack_kernel(labels, band, q_hbm, k_hbm, v_hbm, packed, head_band, sems):
    rows, width = q_hbm.shape
    copies = []
    for slot, head in enumerate(temporal_positions(labels, width // SIZE)):
        head_band[slot] = band[head]
        for tensor, source in enumerate((q_hbm, k_hbm, v_hbm)):
            copies.append(
                pltpu.make_async_copy(
                    source.at[:, pl.ds(pl.multiple_of(head * SIZE, SIZE), SIZE)],
                    packed.at[tensor, pl.ds(slot * rows, rows)],
                    sems.at[tensor, slot],
                )
            )
            copies[-1].start()
    for copy in copies:
        copy.wait()


def place_kernel(labels, spatial_hbm, temporal_hbm, out_hbm, sems):
    rows, width = out_hbm.shape

    def spatial_copy(head):
        columns = pl.ds(pl.multiple_of(head * SIZE, SIZE), SIZE)
        return pltpu.make_async_copy(
            spatial_hbm.at[:, columns], out_hbm.at[:, columns], sems.at[head]
        )

    def start(head, count):
        label = labels[head]

        @pl.when(label == 0)
        def _():
            spatial_copy(head).start()

        @pl.when(label != 0)
        def _():
            columns = pl.ds(pl.multiple_of(head * SIZE, SIZE), SIZE)
            pltpu.make_async_copy(
                temporal_hbm.at[pl.ds(pl.multiple_of(count * rows, UNIT), rows)],
                out_hbm.at[:, columns],
                sems.at[head],
            ).start()

        return count + label

    def finish(head, _):
        spatial_copy(head).wait()
        return 0

    lax.fori_loop(0, width // SIZE, start, jnp.int32(0))
    lax.fori_loop(0, width // SIZE, finish, 0)


def shards(queries, keys, values, labels, band):
    rows, width = queries.shape
    frames = lax.axis_size("frame") // 2
    groups = rows // UNIT
    units = -(-TEMP_HEADS * groups // frames)
    share = units * UNIT
    cuts = len(cut_units(units))
    anywhere = pl.BlockSpec(memory_space=pl.ANY)
    scalars = pl.BlockSpec(memory_space=pltpu.SMEM)
    heads = width // SIZE
    dma = pltpu.SemaphoreType.DMA
    packed, head_band = pl.pallas_call(
        pack_kernel,
        out_shape=(
            jax.ShapeDtypeStruct((3, frames * share, SIZE), BF16),
            jax.ShapeDtypeStruct((TEMP_HEADS,), jnp.int32),
        ),
        in_specs=[scalars, scalars, anywhere, anywhere, anywhere],
        out_specs=(anywhere, scalars),
        scratch_shapes=[dma((3, TEMP_HEADS))],
    )(labels, band, queries, keys, values)
    spatial, temporal = pl.pallas_call(
        functools.partial(kernel, frames, units),
        out_shape=(
            jax.ShapeDtypeStruct((rows, width), BF16),
            jax.ShapeDtypeStruct((frames * share, SIZE), BF16),
        ),
        in_specs=[scalars, anywhere, anywhere, anywhere, anywhere],
        out_specs=(anywhere, anywhere),
        scratch_shapes=[
            pltpu.VMEM((rows, width), BF16),
            pltpu.VMEM((2 * rows, width), BF16),
            pltpu.VMEM((2 * rows, width), BF16),
            pltpu.VMEM((3, frames, share, SIZE), BF16),
            pltpu.VMEM((frames, share, SIZE), BF16),
            pltpu.VMEM((rows, width), BF16),
            dma((3,)),
            dma((2,)),
            dma((2,)),
            dma((3,)),
            dma((cuts, 3, frames)),
            dma((cuts, 3, frames)),
            dma((cuts,)),
            dma((cuts, frames)),
            dma((cuts, frames)),
            dma,
        ],
        compiler_params=pltpu.CompilerParams(
            collective_id=0, has_side_effects=True, vmem_limit_bytes=56 * 2**20
        ),
        cost_estimate=pl.CostEstimate(
            flops=8 * heads * rows * rows * SIZE,
            bytes_accessed=8 * rows * width,
            transcendentals=2 * heads * rows * rows,
        ),
    )(head_band, packed, queries, keys, values)
    return pl.pallas_call(
        place_kernel,
        out_shape=jax.ShapeDtypeStruct((rows, width), BF16),
        in_specs=[scalars, anywhere, anywhere],
        out_specs=anywhere,
        scratch_shapes=[dma((heads,))],
    )(labels, spatial, temporal)


def solution(mesh):
    placed = (
        P(("group", "frame"), None),
        P(("group", "frame"), None),
        P(("group", "frame"), None),
        P("group"),
        P("group"),
    )
    return jax.shard_map(
        shards, mesh=mesh, in_specs=placed, out_specs=P(("group", "frame"), None), check_vma=False
    )
```

```python
import functools
import math

import jax
import jax.numpy as jnp
from jax import lax
from jax.experimental import pallas as pl
from jax.experimental.pallas import tpu as pltpu
from jax.sharding import PartitionSpec as P

TEMP_HEADS = 10
UNIT = 16
SIZE = 128
F32 = jnp.float32
BF16 = jnp.bfloat16


def temporal_positions(labels, heads):
    def pick(head, carry):
        count, found = carry
        label = labels[head]
        found = tuple(
            jnp.where(label * (count + 1) == slot + 1, head, have)
            for slot, have in enumerate(found)
        )
        return count + label, found

    zero = jnp.int32(0)
    return lax.fori_loop(0, heads, pick, (zero, (zero,) * TEMP_HEADS))[1]


def cut_units(units):
    first = (units + 1) // 2
    return [(0, first), (first, units - first)]


def attend(query, key, value, scale, keep=None):
    scores = lax.dot_general(query, key, (((1,), (1,)), ((), ())), preferred_element_type=F32)
    if keep is not None:
        scores = jnp.where(keep, scores, F32(-1e30))
    peak = jnp.max(scores, axis=1, keepdims=True)
    weights = jnp.exp2((scores - peak) * F32(scale * math.log2(math.e))).astype(BF16)
    wide = jnp.concatenate([value, jnp.ones_like(value)], axis=1)
    total = jnp.dot(weights, wide, preferred_element_type=F32)
    return (total[:, :SIZE] / total[:, SIZE:]).astype(BF16)


def kernel(
    frames,
    units,
    head_band,
    packed,
    q_hbm,
    k_hbm,
    v_hbm,
    spatial_hbm,
    temporal_hbm,
    q_own,
    k_all,
    v_all,
    got,
    result,
    spatial,
    load_sem,
    pair_send,
    pair_recv,
    own_sem,
    send_sem,
    recv_sem,
    back_own,
    back_send,
    back_recv,
    out_sem,
):
    rows, width = q_own.shape
    heads = width // SIZE
    groups = rows // UNIT
    share = units * UNIT
    scale = 1.0 / math.sqrt(SIZE)
    cuts = [(start * UNIT, count * UNIT) for start, count in cut_units(units)]
    me = lax.axis_index("frame")
    frame = me // 2
    core = me % 2
    partner = {"frame": me + 1 - 2 * core}

    def peer(other):
        return {"frame": other * 2 + core}

    own_rows = pl.ds(0, rows)
    loads = [
        pltpu.make_async_copy(q_hbm, q_own, load_sem.at[0]),
        pltpu.make_async_copy(k_hbm, k_all.at[own_rows], load_sem.at[1]),
        pltpu.make_async_copy(v_hbm, v_all.at[own_rows], load_sem.at[2]),
    ]
    for load in loads:
        load.start()

    barrier = pltpu.get_barrier_semaphore()
    pl.semaphore_signal(barrier, inc=1, device_id=partner, device_id_type=pl.DeviceIdType.MESH)

    def greet(step, _):
        pl.semaphore_signal(
            barrier,
            inc=1,
            device_id=peer((frame + step) % frames),
            device_id_type=pl.DeviceIdType.MESH,
        )
        return 0

    lax.fori_loop(1, frames, greet, 0)

    pl.semaphore_wait(barrier, frames)

    def part_copy(cut, tensor, to, source):
        first, count = cuts[cut]
        return pltpu.make_async_remote_copy(
            src_ref=packed.at[tensor, pl.ds(pl.multiple_of(to * share + first, UNIT), count)],
            dst_ref=got.at[tensor, frame, pl.ds(first, count)],
            send_sem=send_sem.at[cut, tensor, to],
            recv_sem=recv_sem.at[cut, tensor, source],
            device_id=peer(to),
            device_id_type=pl.DeviceIdType.MESH,
        )

    def own_copy(tensor):
        return pltpu.make_async_copy(
            packed.at[tensor, pl.ds(pl.multiple_of(frame * share, UNIT), share)],
            got.at[tensor, frame],
            own_sem.at[tensor],
        )

    def back_copy(cut, to, source):
        first, count = cuts[cut]
        return pltpu.make_async_remote_copy(
            src_ref=result.at[to, pl.ds(first, count)],
            dst_ref=temporal_hbm.at[pl.ds(pl.multiple_of(frame * share + first, UNIT), count)],
            send_sem=back_send.at[cut, to],
            recv_sem=back_recv.at[cut, source],
            device_id=peer(to),
            device_id_type=pl.DeviceIdType.MESH,
        )

    def back_own_copy(cut):
        first, count = cuts[cut]
        return pltpu.make_async_copy(
            result.at[frame, pl.ds(first, count)],
            temporal_hbm.at[pl.ds(pl.multiple_of(frame * share + first, UNIT), count)],
            back_own.at[cut],
        )

    def over_peers(action):
        def step_action(step, _):
            action((frame + step) % frames)
            return 0

        lax.fori_loop(1, frames, step_action, 0)

    pair = []
    for tensor, held in ((1, k_all), (2, v_all)):
        pair.append(
            pltpu.make_async_remote_copy(
                src_ref=held.at[own_rows],
                dst_ref=held.at[pl.ds(rows, rows)],
                send_sem=pair_send.at[tensor - 1],
                recv_sem=pair_recv.at[tensor - 1],
                device_id=partner,
                device_id_type=pl.DeviceIdType.MESH,
            )
        )

    for tensor in range(3):
        over_peers(lambda other, tensor=tensor: part_copy(0, tensor, other, frame).start())
        own_copy(tensor).start()
    for load in loads:
        load.wait()
    for copy in pair:
        copy.start()
    for cut in range(1, len(cuts)):
        for tensor in range(3):
            over_peers(
                lambda other, cut=cut, tensor=tensor: part_copy(cut, tensor, other, frame).start()
            )
    for copy in pair:
        copy.wait()

    def one_head(head, _):
        columns = pl.ds(pl.multiple_of(head * SIZE, SIZE), SIZE)
        spatial[:, columns] = attend(
            q_own[:, columns], k_all[:, columns], v_all[:, columns], scale
        )
        return 0

    lax.fori_loop(0, heads, one_head, 0)
    out_copy = pltpu.make_async_copy(spatial, spatial_hbm, out_sem)
    out_copy.start()

    for tensor in range(3):
        own_copy(tensor).wait()
    tall = frames * UNIT
    row_id = lax.broadcasted_iota(jnp.int32, (tall, tall), 0)
    column_id = lax.broadcasted_iota(jnp.int32, (tall, tall), 1)
    distance = jnp.where(
        row_id % UNIT == column_id % UNIT, jnp.abs(row_id // UNIT - column_id // UNIT), 2 * frames
    )
    for cut, (first, count) in enumerate(cuts):
        for tensor in range(3):
            over_peers(
                lambda other, cut=cut, tensor=tensor: part_copy(
                    cut, tensor, other, other
                ).wait_recv()
            )

        def one_unit(number, _, first=first):
            start = pl.multiple_of(first + number * UNIT, UNIT)
            place = frame * units + first // UNIT + number
            reach = head_band[jnp.minimum(place // groups, TEMP_HEADS - 1)]
            parts = [got[t, :, pl.ds(start, UNIT), :].reshape(tall, SIZE) for t in range(3)]
            out = attend(*parts, scale, distance <= reach)
            result[:, pl.ds(start, UNIT), :] = out.reshape(frames, UNIT, SIZE)
            return 0

        lax.fori_loop(0, count // UNIT, one_unit, 0)
        over_peers(lambda other, cut=cut: back_copy(cut, other, frame).start())
        back_own_copy(cut).start()

    for cut in range(len(cuts)):
        back_own_copy(cut).wait()
        over_peers(lambda other, cut=cut: back_copy(cut, other, other).wait())
        for tensor in range(3):
            over_peers(
                lambda other, cut=cut, tensor=tensor: part_copy(
                    cut, tensor, other, frame
                ).wait_send()
            )
    out_copy.wait()


def pack_kernel(labels, band, q_hbm, k_hbm, v_hbm, packed, head_band, sems):
    rows, width = q_hbm.shape
    copies = []
    for slot, head in enumerate(temporal_positions(labels, width // SIZE)):
        head_band[slot] = band[head]
        for tensor, source in enumerate((q_hbm, k_hbm, v_hbm)):
            copies.append(
                pltpu.make_async_copy(
                    source.at[:, pl.ds(pl.multiple_of(head * SIZE, SIZE), SIZE)],
                    packed.at[tensor, pl.ds(slot * rows, rows)],
                    sems.at[tensor, slot],
                )
            )
            copies[-1].start()
    for copy in copies:
        copy.wait()


def place_kernel(labels, spatial, temporal, out):
    out[...] = spatial[...]
    heads = out.shape[1] // SIZE
    for slot, head in enumerate(temporal_positions(labels, heads)):
        out[:, pl.ds(pl.multiple_of(head * SIZE, SIZE), SIZE)] = temporal[slot]


def place_rows(rows):
    return next(count for count in (160, 128, 64, 32, 16) if rows % count == 0)


def shards(queries, keys, values, labels, band):
    rows, width = queries.shape
    frames = lax.axis_size("frame") // 2
    groups = rows // UNIT
    units = -(-TEMP_HEADS * groups // frames)
    share = units * UNIT
    cuts = len(cut_units(units))
    anywhere = pl.BlockSpec(memory_space=pl.ANY)
    scalars = pl.BlockSpec(memory_space=pltpu.SMEM)
    heads = width // SIZE
    dma = pltpu.SemaphoreType.DMA
    packed, head_band = pl.pallas_call(
        pack_kernel,
        out_shape=(
            jax.ShapeDtypeStruct((3, frames * share, SIZE), BF16),
            jax.ShapeDtypeStruct((TEMP_HEADS,), jnp.int32),
        ),
        in_specs=[scalars, scalars, anywhere, anywhere, anywhere],
        out_specs=(pl.BlockSpec(memory_space=pltpu.VMEM), scalars),
        scratch_shapes=[dma((3, TEMP_HEADS))],
        compiler_params=pltpu.CompilerParams(vmem_limit_bytes=24 * 2**20),
    )(labels, band, queries, keys, values)
    spatial, temporal = pl.pallas_call(
        functools.partial(kernel, frames, units),
        out_shape=(
            jax.ShapeDtypeStruct((rows, width), BF16),
            jax.ShapeDtypeStruct((frames * share, SIZE), BF16),
        ),
        in_specs=[scalars, anywhere, anywhere, anywhere, anywhere],
        out_specs=(anywhere, anywhere),
        scratch_shapes=[
            pltpu.VMEM((rows, width), BF16),
            pltpu.VMEM((2 * rows, width), BF16),
            pltpu.VMEM((2 * rows, width), BF16),
            pltpu.VMEM((3, frames, share, SIZE), BF16),
            pltpu.VMEM((frames, share, SIZE), BF16),
            pltpu.VMEM((rows, width), BF16),
            dma((3,)),
            dma((2,)),
            dma((2,)),
            dma((3,)),
            dma((cuts, 3, frames)),
            dma((cuts, 3, frames)),
            dma((cuts,)),
            dma((cuts, frames)),
            dma((cuts, frames)),
            dma,
        ],
        compiler_params=pltpu.CompilerParams(
            collective_id=0, has_side_effects=True, vmem_limit_bytes=56 * 2**20
        ),
        cost_estimate=pl.CostEstimate(
            flops=8 * heads * rows * rows * SIZE,
            bytes_accessed=8 * rows * width,
            transcendentals=2 * heads * rows * rows,
        ),
    )(head_band, packed, queries, keys, values)
    block = place_rows(rows)
    return pl.pallas_call(
        place_kernel,
        grid=(rows // block,),
        out_shape=jax.ShapeDtypeStruct((rows, width), BF16),
        in_specs=[
            scalars,
            pl.BlockSpec((block, width), lambda step: (step, 0)),
            pl.BlockSpec((TEMP_HEADS, block, SIZE), lambda step: (0, step, 0)),
        ],
        out_specs=pl.BlockSpec((block, width), lambda step: (step, 0)),
        compiler_params=pltpu.CompilerParams(vmem_limit_bytes=24 * 2**20),
    )(labels, spatial, temporal[: TEMP_HEADS * rows].reshape(TEMP_HEADS, rows, SIZE))


def solution(mesh):
    placed = (
        P(("group", "frame"), None),
        P(("group", "frame"), None),
        P(("group", "frame"), None),
        P("group"),
        P("group"),
    )
    return jax.shard_map(
        shards, mesh=mesh, in_specs=placed, out_specs=P(("group", "frame"), None), check_vma=False
    )
```

```python
import functools
import math

import jax
import jax.numpy as jnp
from jax import lax
from jax.experimental import pallas as pl
from jax.experimental.pallas import tpu as pltpu
from jax.sharding import PartitionSpec as P

TEMP_HEADS = 10
UNIT = 16
BATCH = 4
SIZE = 128
F32 = jnp.float32
BF16 = jnp.bfloat16


def temporal_positions(labels, heads):
    def pick(head, carry):
        count, found = carry
        label = labels[head]
        found = tuple(
            jnp.where(label * (count + 1) == slot + 1, head, have)
            for slot, have in enumerate(found)
        )
        return count + label, found

    zero = jnp.int32(0)
    return lax.fori_loop(0, heads, pick, (zero, (zero,) * TEMP_HEADS))[1]


def cut_units(units):
    first = (units + 1) // 2
    return [(0, first), (first, units - first)]


def attend(query, key, value, scale, keep=None):
    scores = lax.dot_general(query, key, (((1,), (1,)), ((), ())), preferred_element_type=F32)
    if keep is not None:
        scores = jnp.where(keep, scores, F32(-1e30))
    peak = jnp.max(scores, axis=1, keepdims=True)
    weights = jnp.exp2((scores - peak) * F32(scale * math.log2(math.e))).astype(BF16)
    wide = jnp.concatenate([value, jnp.ones_like(value)], axis=1)
    total = jnp.dot(weights, wide, preferred_element_type=F32)
    return (total[:, :SIZE] / total[:, SIZE:]).astype(BF16)


def kernel(
    frames,
    units,
    head_band,
    packed,
    q_hbm,
    k_hbm,
    v_hbm,
    spatial_hbm,
    temporal_hbm,
    q_own,
    k_all,
    v_all,
    got,
    result,
    spatial,
    load_sem,
    pair_send,
    pair_recv,
    own_sem,
    send_sem,
    recv_sem,
    back_own,
    back_send,
    back_recv,
    out_sem,
):
    rows, width = q_own.shape
    heads = width // SIZE
    groups = rows // UNIT
    share = units * UNIT
    scale = 1.0 / math.sqrt(SIZE)
    cuts = [(start * UNIT, count * UNIT) for start, count in cut_units(units)]
    me = lax.axis_index("frame")
    frame = me // 2
    core = me % 2
    partner = {"frame": me + 1 - 2 * core}

    def peer(other):
        return {"frame": other * 2 + core}

    own_rows = pl.ds(0, rows)
    loads = [
        pltpu.make_async_copy(q_hbm, q_own, load_sem.at[0]),
        pltpu.make_async_copy(k_hbm, k_all.at[own_rows], load_sem.at[1]),
        pltpu.make_async_copy(v_hbm, v_all.at[own_rows], load_sem.at[2]),
    ]
    for load in loads:
        load.start()

    barrier = pltpu.get_barrier_semaphore()
    pl.semaphore_signal(barrier, inc=1, device_id=partner, device_id_type=pl.DeviceIdType.MESH)

    def greet(step, _):
        pl.semaphore_signal(
            barrier,
            inc=1,
            device_id=peer((frame + step) % frames),
            device_id_type=pl.DeviceIdType.MESH,
        )
        return 0

    lax.fori_loop(1, frames, greet, 0)

    pl.semaphore_wait(barrier, frames)

    def part_copy(cut, tensor, to, source):
        first, count = cuts[cut]
        return pltpu.make_async_remote_copy(
            src_ref=packed.at[tensor, pl.ds(pl.multiple_of(to * share + first, UNIT), count)],
            dst_ref=got.at[tensor, frame, pl.ds(first, count)],
            send_sem=send_sem.at[cut, tensor, to],
            recv_sem=recv_sem.at[cut, tensor, source],
            device_id=peer(to),
            device_id_type=pl.DeviceIdType.MESH,
        )

    def own_copy(tensor):
        return pltpu.make_async_copy(
            packed.at[tensor, pl.ds(pl.multiple_of(frame * share, UNIT), share)],
            got.at[tensor, frame],
            own_sem.at[tensor],
        )

    def back_copy(cut, to, source):
        first, count = cuts[cut]
        return pltpu.make_async_remote_copy(
            src_ref=result.at[to, pl.ds(first, count)],
            dst_ref=temporal_hbm.at[pl.ds(pl.multiple_of(frame * share + first, UNIT), count)],
            send_sem=back_send.at[cut, to],
            recv_sem=back_recv.at[cut, source],
            device_id=peer(to),
            device_id_type=pl.DeviceIdType.MESH,
        )

    def back_own_copy(cut):
        first, count = cuts[cut]
        return pltpu.make_async_copy(
            result.at[frame, pl.ds(first, count)],
            temporal_hbm.at[pl.ds(pl.multiple_of(frame * share + first, UNIT), count)],
            back_own.at[cut],
        )

    def over_peers(action):
        def step_action(step, _):
            action((frame + step) % frames)
            return 0

        lax.fori_loop(1, frames, step_action, 0)

    pair = []
    for tensor, held in ((1, k_all), (2, v_all)):
        pair.append(
            pltpu.make_async_remote_copy(
                src_ref=held.at[own_rows],
                dst_ref=held.at[pl.ds(rows, rows)],
                send_sem=pair_send.at[tensor - 1],
                recv_sem=pair_recv.at[tensor - 1],
                device_id=partner,
                device_id_type=pl.DeviceIdType.MESH,
            )
        )

    for tensor in range(3):
        over_peers(lambda other, tensor=tensor: part_copy(0, tensor, other, frame).start())
        own_copy(tensor).start()
    for load in loads:
        load.wait()
    for copy in pair:
        copy.start()
    for cut in range(1, len(cuts)):
        for tensor in range(3):
            over_peers(
                lambda other, cut=cut, tensor=tensor: part_copy(cut, tensor, other, frame).start()
            )
    for copy in pair:
        copy.wait()

    def one_head(head, _):
        columns = pl.ds(pl.multiple_of(head * SIZE, SIZE), SIZE)
        spatial[:, columns] = attend(
            q_own[:, columns], k_all[:, columns], v_all[:, columns], scale
        )
        return 0

    lax.fori_loop(0, heads, one_head, 0)
    out_copy = pltpu.make_async_copy(spatial, spatial_hbm, out_sem)
    out_copy.start()

    for tensor in range(3):
        own_copy(tensor).wait()
    tall = frames * UNIT
    row_id = lax.broadcasted_iota(jnp.int32, (tall, tall), 0)
    column_id = lax.broadcasted_iota(jnp.int32, (tall, tall), 1)
    distance = jnp.where(
        row_id % UNIT == column_id % UNIT, jnp.abs(row_id // UNIT - column_id // UNIT), 2 * frames
    )
    for cut, (first, count) in enumerate(cuts):
        for tensor in range(3):
            over_peers(
                lambda other, cut=cut, tensor=tensor: part_copy(
                    cut, tensor, other, other
                ).wait_recv()
            )

        def one_unit(number, first):
            start = pl.multiple_of(first + number * UNIT, UNIT)
            place = frame * units + first // UNIT + number
            reach = head_band[jnp.minimum(place // groups, TEMP_HEADS - 1)]
            parts = [got[t, :, pl.ds(start, UNIT), :].reshape(tall, SIZE) for t in range(3)]
            out = attend(*parts, scale, distance <= reach)
            return start, out.reshape(frames, UNIT, SIZE)

        def some_units(base, size, first):
            for start, out in [one_unit(base + step, first) for step in range(size)]:
                result[:, pl.ds(start, UNIT), :] = out

        def one_batch(number, _, first=first):
            some_units(number * BATCH, BATCH, first)
            return 0

        todo = count // UNIT
        lax.fori_loop(0, todo // BATCH, one_batch, 0)
        if todo % BATCH:
            some_units(todo - todo % BATCH, todo % BATCH, first)
        over_peers(lambda other, cut=cut: back_copy(cut, other, frame).start())
        back_own_copy(cut).start()

    for cut in range(len(cuts)):
        back_own_copy(cut).wait()
        over_peers(lambda other, cut=cut: back_copy(cut, other, other).wait())
        for tensor in range(3):
            over_peers(
                lambda other, cut=cut, tensor=tensor: part_copy(
                    cut, tensor, other, frame
                ).wait_send()
            )
    out_copy.wait()


def pack_kernel(labels, band, q_hbm, k_hbm, v_hbm, packed, head_band, held, in_sem, out_sem):
    rows, width = q_hbm.shape
    found = temporal_positions(labels, width // SIZE)
    copies = []
    for tensor, source in enumerate((q_hbm, k_hbm, v_hbm)):
        for slot, head in enumerate(found):
            copy = pltpu.make_async_copy(
                source.at[:, pl.ds(pl.multiple_of(head * SIZE, SIZE), SIZE)],
                held.at[tensor, pl.ds(slot * rows, rows)],
                in_sem.at[tensor, slot],
            )
            copy.start()
            part = (tensor, pl.ds(slot * rows, rows))
            back = pltpu.make_async_copy(
                held.at[part], packed.at[part], out_sem.at[tensor, slot]
            )
            copies.append((copy, back))
    for slot, head in enumerate(found):
        head_band[slot] = band[head]
    for copy, back in copies:
        copy.wait()
        back.start()
    for _, back in copies:
        back.wait()


def place_kernel(labels, spatial, temporal, out):
    out[...] = spatial[...]
    heads = out.shape[1] // SIZE
    for slot, head in enumerate(temporal_positions(labels, heads)):
        out[:, pl.ds(pl.multiple_of(head * SIZE, SIZE), SIZE)] = temporal[slot]


def place_rows(rows):
    return next(count for count in (64, 32, 16) if rows % count == 0)


def shards(queries, keys, values, labels, band):
    rows, width = queries.shape
    frames = lax.axis_size("frame") // 2
    groups = rows // UNIT
    units = -(-TEMP_HEADS * groups // frames)
    share = units * UNIT
    cuts = len(cut_units(units))
    anywhere = pl.BlockSpec(memory_space=pl.ANY)
    scalars = pl.BlockSpec(memory_space=pltpu.SMEM)
    heads = width // SIZE
    dma = pltpu.SemaphoreType.DMA
    packed, head_band = pl.pallas_call(
        pack_kernel,
        out_shape=(
            jax.ShapeDtypeStruct((3, frames * share, SIZE), BF16),
            jax.ShapeDtypeStruct((TEMP_HEADS,), jnp.int32),
        ),
        in_specs=[scalars, scalars, anywhere, anywhere, anywhere],
        out_specs=(anywhere, scalars),
        scratch_shapes=[
            pltpu.VMEM((3, TEMP_HEADS * rows, SIZE), BF16),
            dma((3, TEMP_HEADS)),
            dma((3, TEMP_HEADS)),
        ],
        compiler_params=pltpu.CompilerParams(vmem_limit_bytes=56 * 2**20),
    )(labels, band, queries, keys, values)
    spatial, temporal = pl.pallas_call(
        functools.partial(kernel, frames, units),
        out_shape=(
            jax.ShapeDtypeStruct((rows, width), BF16),
            jax.ShapeDtypeStruct((frames * share, SIZE), BF16),
        ),
        in_specs=[scalars, anywhere, anywhere, anywhere, anywhere],
        out_specs=(anywhere, anywhere),
        scratch_shapes=[
            pltpu.VMEM((rows, width), BF16),
            pltpu.VMEM((2 * rows, width), BF16),
            pltpu.VMEM((2 * rows, width), BF16),
            pltpu.VMEM((3, frames, share, SIZE), BF16),
            pltpu.VMEM((frames, share, SIZE), BF16),
            pltpu.VMEM((rows, width), BF16),
            dma((3,)),
            dma((2,)),
            dma((2,)),
            dma((3,)),
            dma((cuts, 3, frames)),
            dma((cuts, 3, frames)),
            dma((cuts,)),
            dma((cuts, frames)),
            dma((cuts, frames)),
            dma,
        ],
        compiler_params=pltpu.CompilerParams(
            collective_id=0, has_side_effects=True, vmem_limit_bytes=56 * 2**20
        ),
        cost_estimate=pl.CostEstimate(
            flops=8 * heads * rows * rows * SIZE,
            bytes_accessed=8 * rows * width,
            transcendentals=2 * heads * rows * rows,
        ),
    )(head_band, packed, queries, keys, values)
    block = place_rows(rows)
    return pl.pallas_call(
        place_kernel,
        grid=(rows // block,),
        out_shape=jax.ShapeDtypeStruct((rows, width), BF16),
        in_specs=[
            scalars,
            pl.BlockSpec((block, width), lambda step: (step, 0)),
            pl.BlockSpec((TEMP_HEADS, block, SIZE), lambda step: (0, step, 0)),
        ],
        out_specs=pl.BlockSpec((block, width), lambda step: (step, 0)),
        compiler_params=pltpu.CompilerParams(vmem_limit_bytes=56 * 2**20),
    )(labels, spatial, temporal[: TEMP_HEADS * rows].reshape(TEMP_HEADS, rows, SIZE))


def solution(mesh):
    placed = (
        P(("group", "frame"), None),
        P(("group", "frame"), None),
        P(("group", "frame"), None),
        P("group"),
        P("group"),
    )
    return jax.shard_map(
        shards, mesh=mesh, in_specs=placed, out_specs=P(("group", "frame"), None), check_vma=False
    )
```

```python
import functools
import math

import jax
import jax.numpy as jnp
from jax import lax
from jax.experimental import pallas as pl
from jax.experimental.pallas import tpu as pltpu
from jax.sharding import PartitionSpec as P

TEMP_HEADS = 10
UNIT = 16
CUTS = (13, 12)
BATCH = 4
SIZE = 128
F32 = jnp.float32
BF16 = jnp.bfloat16


def cut_units(units):
    cuts, start = [], 0
    for number, weight in enumerate(CUTS):
        left = units - start
        size = left if number == len(CUTS) - 1 else min(left, -(-units * weight // sum(CUTS)))
        if size:
            cuts.append((start, size))
        start += size
    return cuts


def attend(query, key, value, scale, keep=None):
    scores = lax.dot_general(query, key, (((1,), (1,)), ((), ())), preferred_element_type=F32)
    if keep is not None:
        scores = jnp.where(keep, scores, F32(-1e30))
    peak = jnp.max(scores, axis=1, keepdims=True)
    weights = jnp.exp2((scores - peak) * F32(scale * math.log2(math.e))).astype(BF16)
    wide = jnp.concatenate([value, jnp.ones_like(value)], axis=1)
    total = jnp.dot(weights, wide, preferred_element_type=F32)
    return (total[:, :SIZE] / total[:, SIZE:]).astype(BF16)


def kernel(
    frames,
    units,
    head_band,
    packed,
    q_hbm,
    k_hbm,
    v_hbm,
    spatial_hbm,
    temporal_hbm,
    q_own,
    k_all,
    v_all,
    got,
    result,
    spatial,
    load_sem,
    pair_send,
    pair_recv,
    own_sem,
    send_sem,
    recv_sem,
    back_own,
    back_send,
    back_recv,
    out_sem,
):
    rows, width = q_own.shape
    heads = width // SIZE
    groups = rows // UNIT
    share = units * UNIT
    scale = 1.0 / math.sqrt(SIZE)
    cuts = [(start * UNIT, count * UNIT) for start, count in cut_units(units)]
    me = lax.axis_index("frame")
    frame = me // 2
    core = me % 2
    partner = {"frame": me + 1 - 2 * core}

    def peer(other):
        return {"frame": other * 2 + core}

    own_rows = pl.ds(0, rows)
    loads = [
        pltpu.make_async_copy(q_hbm, q_own, load_sem.at[0]),
        pltpu.make_async_copy(k_hbm, k_all.at[own_rows], load_sem.at[1]),
        pltpu.make_async_copy(v_hbm, v_all.at[own_rows], load_sem.at[2]),
    ]
    for load in loads:
        load.start()

    barrier = pltpu.get_barrier_semaphore()
    pl.semaphore_signal(barrier, inc=1, device_id=partner, device_id_type=pl.DeviceIdType.MESH)

    def greet(step, _):
        pl.semaphore_signal(
            barrier,
            inc=1,
            device_id=peer((frame + step) % frames),
            device_id_type=pl.DeviceIdType.MESH,
        )
        return 0

    lax.fori_loop(1, frames, greet, 0)

    pl.semaphore_wait(barrier, frames)

    def part_copy(cut, tensor, to, source):
        first, count = cuts[cut]
        return pltpu.make_async_remote_copy(
            src_ref=packed.at[tensor, pl.ds(pl.multiple_of(to * share + first, UNIT), count)],
            dst_ref=got.at[tensor, frame, pl.ds(first, count)],
            send_sem=send_sem.at[cut, tensor, to],
            recv_sem=recv_sem.at[cut, tensor, source],
            device_id=peer(to),
            device_id_type=pl.DeviceIdType.MESH,
        )

    def own_copy(tensor):
        return pltpu.make_async_copy(
            packed.at[tensor, pl.ds(pl.multiple_of(frame * share, UNIT), share)],
            got.at[tensor, frame],
            own_sem.at[tensor],
        )

    def back_copy(cut, to, source):
        first, count = cuts[cut]
        return pltpu.make_async_remote_copy(
            src_ref=result.at[to, pl.ds(first, count)],
            dst_ref=temporal_hbm.at[pl.ds(pl.multiple_of(frame * share + first, UNIT), count)],
            send_sem=back_send.at[cut, to],
            recv_sem=back_recv.at[cut, source],
            device_id=peer(to),
            device_id_type=pl.DeviceIdType.MESH,
        )

    def back_own_copy(cut):
        first, count = cuts[cut]
        return pltpu.make_async_copy(
            result.at[frame, pl.ds(first, count)],
            temporal_hbm.at[pl.ds(pl.multiple_of(frame * share + first, UNIT), count)],
            back_own.at[cut],
        )

    def over_peers(action):
        def step_action(step, _):
            action((frame + step) % frames)
            return 0

        lax.fori_loop(1, frames, step_action, 0)

    pair = []
    for tensor, held in ((1, k_all), (2, v_all)):
        pair.append(
            pltpu.make_async_remote_copy(
                src_ref=held.at[own_rows],
                dst_ref=held.at[pl.ds(rows, rows)],
                send_sem=pair_send.at[tensor - 1],
                recv_sem=pair_recv.at[tensor - 1],
                device_id=partner,
                device_id_type=pl.DeviceIdType.MESH,
            )
        )

    for tensor in range(3):
        over_peers(lambda other, tensor=tensor: part_copy(0, tensor, other, frame).start())
        own_copy(tensor).start()
    for load in loads:
        load.wait()
    for copy in pair:
        copy.start()
    for cut in range(1, len(cuts)):
        for tensor in range(3):
            over_peers(
                lambda other, cut=cut, tensor=tensor: part_copy(cut, tensor, other, frame).start()
            )
    for copy in pair:
        copy.wait()

    def one_head(head, _):
        columns = pl.ds(pl.multiple_of(head * SIZE, SIZE), SIZE)
        spatial[:, columns] = attend(
            q_own[:, columns], k_all[:, columns], v_all[:, columns], scale
        )
        return 0

    lax.fori_loop(0, heads, one_head, 0)
    out_copy = pltpu.make_async_copy(spatial, spatial_hbm, out_sem)
    out_copy.start()

    for tensor in range(3):
        own_copy(tensor).wait()
    tall = frames * UNIT
    row_id = lax.broadcasted_iota(jnp.int32, (tall, tall), 0)
    column_id = lax.broadcasted_iota(jnp.int32, (tall, tall), 1)
    distance = jnp.where(
        row_id % UNIT == column_id % UNIT, jnp.abs(row_id // UNIT - column_id // UNIT), 2 * frames
    )
    for cut, (first, count) in enumerate(cuts):
        for tensor in range(3):
            over_peers(
                lambda other, cut=cut, tensor=tensor: part_copy(
                    cut, tensor, other, other
                ).wait_recv()
            )

        def one_unit(number, first):
            start = pl.multiple_of(first + number * UNIT, UNIT)
            place = frame * units + first // UNIT + number
            reach = head_band[jnp.minimum(place // groups, TEMP_HEADS - 1)]
            parts = [got[t, :, pl.ds(start, UNIT), :].reshape(tall, SIZE) for t in range(3)]
            out = attend(*parts, scale, distance <= reach)
            return start, out.reshape(frames, UNIT, SIZE)

        def some_units(base, size, first):
            for start, out in [one_unit(base + step, first) for step in range(size)]:
                result[:, pl.ds(start, UNIT), :] = out

        def one_batch(number, _, first=first):
            some_units(number * BATCH, BATCH, first)
            return 0

        todo = count // UNIT
        lax.fori_loop(0, todo // BATCH, one_batch, 0)
        if todo % BATCH:
            some_units(todo - todo % BATCH, todo % BATCH, first)
        over_peers(lambda other, cut=cut: back_copy(cut, other, frame).start())
        back_own_copy(cut).start()

    for cut in range(len(cuts)):
        back_own_copy(cut).wait()
        over_peers(lambda other, cut=cut: back_copy(cut, other, other).wait())
        for tensor in range(3):
            over_peers(
                lambda other, cut=cut, tensor=tensor: part_copy(
                    cut, tensor, other, frame
                ).wait_send()
            )
    out_copy.wait()


def pack_kernel(labels, band, q_hbm, k_hbm, v_hbm, packed, head_band, found, held, in_sem, out_sem):
    rows, width = q_hbm.shape

    def pick(head, count):
        found[count] = head
        return count + labels[head]

    lax.fori_loop(0, width // SIZE, pick, jnp.int32(0), unroll=True)
    copies = []
    for tensor, source in enumerate((q_hbm, k_hbm, v_hbm)):
        for slot in range(TEMP_HEADS):
            head = found[slot]
            copy = pltpu.make_async_copy(
                source.at[:, pl.ds(pl.multiple_of(head * SIZE, SIZE), SIZE)],
                held.at[tensor, pl.ds(slot * rows, rows)],
                in_sem.at[tensor, slot],
            )
            copy.start()
            part = (tensor, pl.ds(slot * rows, rows))
            back = pltpu.make_async_copy(
                held.at[part], packed.at[part], out_sem.at[tensor, slot]
            )
            copies.append((copy, back))
    for slot in range(TEMP_HEADS):
        head_band[slot] = band[found[slot]]
    for copy, back in copies:
        copy.wait()
        back.start()
    for _, back in copies:
        back.wait()


def place_kernel(found, spatial_hbm, temporal_hbm, out_hbm, held, temporal, first_sem, in_sem, out_sem):
    rows = held.shape[0]
    blocks = in_sem.shape[0]
    block = rows // blocks
    parts = [pl.ds(number * block, block) for number in range(blocks)]
    arrive = pltpu.make_async_copy(
        temporal_hbm.at[pl.ds(0, TEMP_HEADS * rows)], temporal, first_sem
    )
    arrive.start()
    loads = [
        pltpu.make_async_copy(spatial_hbm.at[part], held.at[part], in_sem.at[number])
        for number, part in enumerate(parts)
    ]
    stores = [
        pltpu.make_async_copy(held.at[part], out_hbm.at[part], out_sem.at[number])
        for number, part in enumerate(parts)
    ]
    for load in loads:
        load.start()
    arrive.wait()
    for number, part in enumerate(parts):
        loads[number].wait()
        for slot in range(TEMP_HEADS):
            columns = pl.ds(pl.multiple_of(found[slot] * SIZE, SIZE), SIZE)
            held[part, columns] = temporal[pl.ds(slot * rows + number * block, block)]
        stores[number].start()
    for store in stores:
        store.wait()


def place_blocks(rows):
    return next(count for count in (5, 4, 2, 1) if rows % (count * UNIT) == 0)


def shards(queries, keys, values, labels, band):
    rows, width = queries.shape
    frames = lax.axis_size("frame") // 2
    groups = rows // UNIT
    units = -(-TEMP_HEADS * groups // frames)
    share = units * UNIT
    cuts = len(cut_units(units))
    anywhere = pl.BlockSpec(memory_space=pl.ANY)
    scalars = pl.BlockSpec(memory_space=pltpu.SMEM)
    heads = width // SIZE
    dma = pltpu.SemaphoreType.DMA
    packed, head_band, found = pl.pallas_call(
        pack_kernel,
        out_shape=(
            jax.ShapeDtypeStruct((3, frames * share, SIZE), BF16),
            jax.ShapeDtypeStruct((TEMP_HEADS,), jnp.int32),
            jax.ShapeDtypeStruct((TEMP_HEADS + 1,), jnp.int32),
        ),
        in_specs=[scalars, scalars, anywhere, anywhere, anywhere],
        out_specs=(anywhere, scalars, scalars),
        scratch_shapes=[
            pltpu.VMEM((3, TEMP_HEADS * rows, SIZE), BF16),
            dma((3, TEMP_HEADS)),
            dma((3, TEMP_HEADS)),
        ],
        compiler_params=pltpu.CompilerParams(vmem_limit_bytes=56 * 2**20),
    )(labels, band, queries, keys, values)
    spatial, temporal = pl.pallas_call(
        functools.partial(kernel, frames, units),
        out_shape=(
            jax.ShapeDtypeStruct((rows, width), BF16),
            jax.ShapeDtypeStruct((frames * share, SIZE), BF16),
        ),
        in_specs=[scalars, anywhere, anywhere, anywhere, anywhere],
        out_specs=(anywhere, anywhere),
        scratch_shapes=[
            pltpu.VMEM((rows, width), BF16),
            pltpu.VMEM((2 * rows, width), BF16),
            pltpu.VMEM((2 * rows, width), BF16),
            pltpu.VMEM((3, frames, share, SIZE), BF16),
            pltpu.VMEM((frames, share, SIZE), BF16),
            pltpu.VMEM((rows, width), BF16),
            dma((3,)),
            dma((2,)),
            dma((2,)),
            dma((3,)),
            dma((cuts, 3, frames)),
            dma((cuts, 3, frames)),
            dma((cuts,)),
            dma((cuts, frames)),
            dma((cuts, frames)),
            dma,
        ],
        compiler_params=pltpu.CompilerParams(
            collective_id=0, has_side_effects=True, vmem_limit_bytes=56 * 2**20
        ),
        cost_estimate=pl.CostEstimate(
            flops=8 * heads * rows * rows * SIZE,
            bytes_accessed=8 * rows * width,
            transcendentals=2 * heads * rows * rows,
        ),
    )(head_band, packed, queries, keys, values)
    blocks = place_blocks(rows)
    return pl.pallas_call(
        place_kernel,
        out_shape=jax.ShapeDtypeStruct((rows, width), BF16),
        in_specs=[scalars, anywhere, anywhere],
        out_specs=anywhere,
        scratch_shapes=[
            pltpu.VMEM((rows, width), BF16),
            pltpu.VMEM((TEMP_HEADS * rows, SIZE), BF16),
            dma,
            dma((blocks,)),
            dma((blocks,)),
        ],
        compiler_params=pltpu.CompilerParams(vmem_limit_bytes=56 * 2**20),
    )(found, spatial, temporal)


def solution(mesh):
    placed = (
        P(("group", "frame"), None),
        P(("group", "frame"), None),
        P(("group", "frame"), None),
        P("group"),
        P("group"),
    )
    return jax.shard_map(
        shards, mesh=mesh, in_specs=placed, out_specs=P(("group", "frame"), None), check_vma=False
    )
```
